1024 devices in a mesh: dp: 16 (over z_lo, x), expert: 64 (over y, z_hi, core).
Axes of the slice: x: 4, y: 8, z: 16 (z_hi: 4, z_lo: 4; z = z_hi * 4 + z_lo), core: 2. Of those that a mesh axis runs over, the one named last changes fastest.
Arguments:
- compressed_tokens: bfloat16 [262144, 512], P(('dp', 'expert')), may hold values from -6 to 6
- picked_specialists: int32 [262144, 8], P(('dp', 'expert')), may hold values from 0 to 255, all different within a row
- gating_shares: float32 [262144, 8], P(('dp', 'expert')), may hold values from 0.05 to 0.3
- seat_limits: int32 [64], replicated, may hold values from 4 to 8, as said below
- raising_factors: bfloat16 [64, 512, 1024], P('expert', 'dp'), may hold values from -0.25 to 0.25
- lowering_factors: bfloat16 [64, 512, 1024], P('expert', 'dp'), may hold values from -0.1875 to 0.1875
- result_cotangent: bfloat16 [262144, 512], P(('dp', 'expert')), may hold values from -6 to 6
Outputs:
- combined: bfloat16 [262144, 512], P(('dp', 'expert'))
- latent_grad: bfloat16 [262144, 512], P(('dp', 'expert'))
- prob_grad: float32 [262144, 8], P(('dp', 'expert'))
- up_weight_grad: float32 [64, 512, 1024], P('expert', 'dp')
- down_weight_grad: float32 [64, 512, 1024], P('expert', 'dp')
The draws below stay inside these ranges and needn't reach their ends.
Inputs may be any that keep to these rules, and one draw needn't show every extreme that they name: `picked_specialists`: each row names 8 different experts; experts 64 and above are not in flight. `seat_limits`: at least one expert has capacity 8 and at least one has half of 8.
All inputs are finite; a program needn't handle non-finite values.
Results may differ from the reference program's by a relative error of at most 0.02.
Values may be sent and summed in bfloat16 or wider, within the bound.
A program may use at most 32 MiB of HBM per device.

```python
import jax
import jax.numpy as jnp
from jax import lax

LAT = 512
HID = 1024
EXPERTS = 256
TOP = 8
CAP = 8
TOK_DEV = 256
FLIGHT = 64
TOKENS = 262144
N_DP = 16
N_EXPERT = 64


def draw_seat_limits(key, part):
    key = jax.random.fold_in(key, 7)
    first_key, second_key, third_key = jax.random.split(key, 3)
    values = jax.random.randint(first_key, (FLIGHT,), CAP // 2, CAP + 1)
    full_at = jax.random.randint(second_key, (), 0, FLIGHT)
    low_at = (full_at + 1 + jax.random.randint(third_key, (), 0, FLIGHT - 1)) % FLIGHT
    specialist_range = jnp.arange(FLIGHT)
    values = jnp.where(specialist_range == full_at, CAP, values)
    values = jnp.where(specialist_range == low_at, CAP // 2, values)
    return values.astype(jnp.int32)


def levels(stream_key, extent, pieces, least, top_value):
    level = 1.0
    for dim, blocks in pieces:
        heights = jax.random.uniform(jax.random.fold_in(jax.random.fold_in(stream_key, 6), dim), (blocks,), jnp.float32, least / len(pieces), top_value / len(pieces))
        level = level * jnp.repeat(jnp.exp(heights), extent[dim] // blocks).reshape((-1,) + (1,) * (len(extent) - 1 - dim))
    return level


def distinct(key, rows, number_of, top, lift):
    sequence = jax.random.permutation(jax.random.fold_in(key, 1), number_of)
    boost = sequence
    for power in range(3):
        boost = boost * boost // number_of
    boost = boost * lift // number_of
    tickets = jax.random.randint(jax.random.fold_in(key, 2), (rows, number_of), 0, 4096) + boost
    sure = jax.random.permutation(jax.random.fold_in(key, 3), rows)[jnp.arange(number_of) % rows]
    tickets = jnp.where(jnp.arange(rows)[:, None] == sure[None, :], 1 << 14, tickets)
    priority = tickets * number_of + jnp.arange(number_of)
    return lax.top_k(priority.astype(jnp.int32), top)[1].astype(jnp.int32)


def normal_values(key, shape, deviation, most, shards=(), kind=jnp.bfloat16):
    loudness = levels(key, shape, shards, -0.22, 0.18) if shards else 1.0
    entries = jax.random.normal(key, shape, jnp.float32) * deviation * loudness
    return jnp.minimum(jnp.maximum(entries, -most), most).astype(kind)


def setup_inputs(seed: int = 0) -> dict:
    key_list = jax.random.split(jax.random.key(seed), 8)
    compressed_tokens = normal_values(key_list[0], (TOKENS, LAT), 1.0, 6.0, ((0, 1024),))
    picked_specialists = distinct(key_list[1], TOKENS, EXPERTS, TOP, 256)
    gating_shares = jnp.clip(0.05 + 0.25 * jax.random.uniform(key_list[2], (TOKENS, TOP), jnp.float32) ** levels(key_list[2], (TOKENS, TOP), ((0, 1024),), -0.2, 0.2), 0.05, 0.3)
    seat_limits = draw_seat_limits(jax.random.fold_in(key_list[7], 71), 0)
    raising_factors = normal_values(key_list[4], (FLIGHT, LAT, HID), LAT ** -0.5, 0.25, ((0, 64), (1, 16)))
    lowering_factors = normal_values(key_list[5], (FLIGHT, LAT, HID), HID ** -0.5, 0.1875, ((0, 64), (1, 16)))
    result_cotangent = normal_values(key_list[6], (TOKENS, LAT), 1.0, 6.0, ((0, 1024),))
    return dict(compressed_tokens=compressed_tokens, picked_specialists=picked_specialists, gating_shares=gating_shares, seat_limits=seat_limits, raising_factors=raising_factors, lowering_factors=lowering_factors, result_cotangent=result_cotangent)


def assigned_seat(picked_specialists, seat_limits):
    flattened_ids = picked_specialists.reshape(-1).astype(jnp.int32)
    path_total = flattened_ids.shape[0]
    specialist_range = jnp.arange(FLIGHT, dtype=jnp.int32)
    indicator_table = (flattened_ids[:, None] == specialist_range[None, :]).astype(jnp.int32)
    before = jnp.cumsum(indicator_table, axis=0, dtype=jnp.int32) - indicator_table
    ordinal_place = jnp.sum(before * indicator_table, axis=1, dtype=jnp.int32)
    seat_table = jnp.sum(indicator_table * seat_limits[None, :].astype(jnp.int32), axis=1, dtype=jnp.int32)
    admitted_flags = (flattened_ids < FLIGHT) & (ordinal_place < seat_table)
    seat_number = jnp.where(admitted_flags, flattened_ids * CAP + ordinal_place, FLIGHT * CAP).astype(jnp.int32)
    seat_occupant = jnp.full((FLIGHT * CAP,), path_total, jnp.int32)
    seat_occupant = seat_occupant.at[seat_number].set(jnp.arange(path_total, dtype=jnp.int32), mode="drop")
    return admitted_flags, jnp.minimum(seat_number, FLIGHT * CAP - 1), seat_occupant


def pack_rows(values, row_index, filled):
    picked = values[jnp.minimum(row_index, values.shape[0] - 1)]
    return jnp.where(filled[:, None], picked, jnp.zeros_like(picked))


def to_experts(rows):
    reformed_array = rows.reshape(N_EXPERT, FLIGHT, CAP, LAT).transpose(1, 0, 2, 3)
    return reformed_array.reshape(FLIGHT, N_EXPERT * CAP, LAT)


def to_sources(rows):
    reformed_array = rows.reshape(FLIGHT, N_EXPERT, CAP, LAT).transpose(1, 0, 2, 3)
    return reformed_array.reshape(N_EXPERT, FLIGHT * CAP, LAT)


def rounded(values):
    return lax.optimization_barrier(values.astype(jnp.bfloat16)).astype(jnp.float32)


def reference(compressed_tokens, picked_specialists, gating_shares, seat_limits, raising_factors, lowering_factors, result_cotangent):
    path_total = TOK_DEV * TOP
    up_full = raising_factors.astype(jnp.float32)
    down_full = lowering_factors.astype(jnp.float32)

    def group_step(running, inputs):
        latent_group, ids_group, probs_group, grad_group = inputs
        source_rows = latent_group.reshape(N_EXPERT, TOK_DEV, LAT)
        sender_item = ids_group.reshape(N_EXPERT, TOK_DEV, TOP)
        admitted_flags, seat_number, seat_occupant = jax.vmap(lambda specialist_ids: assigned_seat(specialist_ids, seat_limits))(sender_item)
        filled = seat_occupant < path_total
        dispatch_entries = jax.vmap(pack_rows)(source_rows, seat_occupant // TOP, filled)
        incoming_entries = to_experts(dispatch_entries)
        preact = jnp.einsum("erl,elh->erh", incoming_entries.astype(jnp.float32), up_full)
        active = jnp.maximum(preact, 0.0)
        hidden = (active * active).astype(jnp.bfloat16)
        specialist_result = jnp.einsum("erh,elh->erl", hidden.astype(jnp.float32), down_full).astype(jnp.bfloat16)
        homeward_entries = to_sources(specialist_result)
        route_out = jax.vmap(lambda rows, where: rows[where])(homeward_entries, seat_number).astype(jnp.float32)
        route_weight = jnp.where(admitted_flags, probs_group.reshape(N_EXPERT, path_total), 0.0)
        combined = jnp.sum((route_weight[..., None] * route_out).reshape(N_EXPERT, TOK_DEV, TOP, LAT), axis=2)
        grad_rows_f = grad_group.reshape(N_EXPERT, TOK_DEV, LAT).astype(jnp.float32)
        dots = jnp.einsum("stl,stkl->stk", grad_rows_f, route_out.reshape(N_EXPERT, TOK_DEV, TOP, LAT))
        prob_grad = jnp.where(admitted_flags.reshape(N_EXPERT, TOK_DEV, TOP), dots, 0.0)
        route_grad = (route_weight.reshape(N_EXPERT, TOK_DEV, TOP)[..., None] * grad_rows_f[:, :, None, :])
        route_grad = route_grad.reshape(N_EXPERT, path_total, LAT).astype(jnp.bfloat16)
        cotangent_dispatch = jax.vmap(pack_rows)(route_grad, seat_occupant, filled)
        cotangent_entering = to_experts(cotangent_dispatch)
        hidden_grad = jnp.einsum("erl,elh->erh", cotangent_entering.astype(jnp.float32), down_full)
        act_grad = (2.0 * active * hidden_grad).astype(jnp.bfloat16)
        entry_cotangent = jnp.einsum("erh,elh->erl", act_grad.astype(jnp.float32), up_full).astype(jnp.bfloat16)
        cotangent_return = to_sources(entry_cotangent)
        route_dx = jax.vmap(lambda rows, where: rows[where])(cotangent_return, seat_number).astype(jnp.float32)
        route_dx = route_dx * admitted_flags[..., None].astype(jnp.float32)
        latent_grad = jnp.sum(route_dx.reshape(N_EXPERT, TOK_DEV, TOP, LAT), axis=2)
        up_term = rounded(jnp.einsum("erl,erh->elh", incoming_entries.astype(jnp.float32), act_grad.astype(jnp.float32)))
        down_term = rounded(jnp.einsum("erl,erh->elh", cotangent_entering.astype(jnp.float32), hidden.astype(jnp.float32)))
        running = (running[0] + up_term, running[1] + down_term)
        outputs = (combined.reshape(N_EXPERT * TOK_DEV, LAT).astype(jnp.bfloat16),
                   latent_grad.reshape(N_EXPERT * TOK_DEV, LAT).astype(jnp.bfloat16),
                   prob_grad.reshape(N_EXPERT * TOK_DEV, TOP))
        return running, outputs

    block = N_EXPERT * TOK_DEV
    inputs = (compressed_tokens.reshape(N_DP, block, LAT), picked_specialists.reshape(N_DP, block, TOP),
              gating_shares.reshape(N_DP, block, TOP), result_cotangent.reshape(N_DP, block, LAT))
    start = (jnp.zeros((FLIGHT, LAT, HID), jnp.float32), jnp.zeros((FLIGHT, LAT, HID), jnp.float32))
    sums, outputs = lax.scan(group_step, start, inputs)
    combined = outputs[0].reshape(TOKENS, LAT)
    latent_grad = outputs[1].reshape(TOKENS, LAT)
    prob_grad = outputs[2].reshape(TOKENS, TOP)
    return combined, latent_grad, prob_grad, sums[0], sums[1]
```

```python
import functools

import jax
import jax.numpy as jnp
from jax import lax
from jax.experimental import pallas as pl
from jax.experimental.pallas import tpu as pltpu
from jax.sharding import PartitionSpec as P

DP_GRID = (4, 4)
EXPERT_GRID = (8, 4, 2)
SEATS = 8
PAIR = 2 * SEATS
COLUMNS = 256
MESH = pl.DeviceIdType.MESH
BF16 = jnp.bfloat16
F32 = jnp.float32


def dot(a, b):
    return jnp.dot(a, b, preferred_element_type=F32)


def dot_nt(a, b):
    return lax.dot_general(a, b, (((1,), (1,)), ((), ())), preferred_element_type=F32)


def dot_tn(a, b):
    return lax.dot_general(a, b, (((0,), (0,)), ((), ())), preferred_element_type=F32)


def parts_of(values):
    first = values.astype(BF16)
    rest = values - first.astype(F32)
    second = rest.astype(BF16)
    third = (rest - second.astype(F32)).astype(BF16)
    return first, second, third


def paired(upper, lower, blocks):
    width = upper.shape[-1]
    return jnp.concatenate(
        [upper.reshape(blocks, SEATS, width), lower.reshape(blocks, SEATS, width)], axis=1
    ).astype(BF16)


def unpaired(blocks):
    count, _, width = blocks.shape
    wide = blocks.astype(F32)
    return (
        wide[:, :SEATS].reshape(count * SEATS, width),
        wide[:, SEATS:].reshape(count * SEATS, width),
    )


def kernel(
    tok_ref, pick_ref, share_ref, limit_ref, up_ref, down_ref, cot_ref,
    comb_ref, lat_ref, prob_ref, up_grad_ref, down_grad_ref,
    weights, outbox, inbox, reply, home, place, cot_rows, row_share,
    xs, gs, hs, acts, partial, x_in, z_out, z_in,
    ag_z_send, ag_z_recv, ag_x_send, ag_x_recv,
    row_send, row_recv, back_send, back_recv, self_sem,
    rs_x_send, rs_x_recv, rs_z_send, rs_z_recv,
):
    runs, wide = DP_GRID
    ys, stretches, cores = EXPERT_GRID
    experts = ys * stretches * cores
    members = ys * cores
    tokens, lat = tok_ref.shape
    top = pick_ref.shape[1]
    hid = weights.shape[-1]
    slots = experts * SEATS
    group_rows = members * SEATS

    dp = lax.axis_index("dp")
    me = lax.axis_index("expert")
    run, across = dp // wide, dp % wide
    my_y = me // (stretches * cores)
    my_stretch = (me // cores) % stretches
    my_core = me % cores
    my_member = my_y * cores + my_core

    def run_peer(j):
        return {"dp": lax.rem(run + j, runs) * wide + across}

    def wide_peer(j):
        return {"dp": run * wide + lax.rem(across + j, wide)}

    def expert_at(stretch_step, member_step):
        stretch = lax.rem(my_stretch + stretch_step, stretches)
        member = lax.rem(my_member + member_step, members)
        return ((member // cores) * stretches + stretch) * cores + lax.rem(member, cores), member

    barrier = pltpu.get_barrier_semaphore()

    def greet(i, carry):
        pl.semaphore_signal(
            barrier, inc=1, device_id={"expert": lax.rem(me + i, experts)}, device_id_type=MESH
        )
        return carry

    for j in range(1, runs):
        pl.semaphore_signal(barrier, inc=1, device_id=run_peer(j), device_id_type=MESH)
    for j in range(1, wide):
        pl.semaphore_signal(barrier, inc=1, device_id=wide_peer(j), device_id_type=MESH)
    lax.fori_loop(1, experts, greet, 0)

    weights[0, run, across] = up_ref[0]
    weights[1, run, across] = down_ref[0]

    picks = pick_ref[...]
    shares = share_ref[...]
    expert_lane = lax.broadcasted_iota(jnp.int32, (tokens, experts), 1)
    named = jnp.zeros((tokens, experts), F32)
    weight = jnp.zeros((tokens, experts), F32)
    for k in range(top):
        hit = picks[:, k : k + 1] == expert_lane
        named = jnp.where(hit, 1.0, named)
        weight = jnp.where(hit, shares[:, k : k + 1], weight)
    earlier = (
        lax.broadcasted_iota(jnp.int32, (tokens, tokens), 1)
        < lax.broadcasted_iota(jnp.int32, (tokens, tokens), 0)
    ).astype(BF16)
    position = dot(earlier, named.astype(BF16))
    seated = (named > 0.0) & (position < limit_ref[...].astype(F32))
    seat = jnp.where(seated, position, -1.0).astype(BF16)
    spread = (
        lax.broadcasted_iota(jnp.int32, (experts, slots), 1) // SEATS
        == lax.broadcasted_iota(jnp.int32, (experts, slots), 0)
    ).astype(BF16)
    slot_seat = (lax.broadcasted_iota(jnp.int32, (tokens, slots), 1) % SEATS).astype(F32)
    place[...] = (dot(seat, spread) == slot_seat).astype(BF16)
    slot_expert = (
        lax.broadcasted_iota(jnp.int32, (slots, experts), 0) // SEATS
        == lax.broadcasted_iota(jnp.int32, (slots, experts), 1)
    )

    pl.semaphore_wait(barrier, experts - 1 + runs - 1 + wide - 1)

    z_copies = []
    for j in range(1, runs):
        copy = pltpu.make_async_remote_copy(
            src_ref=weights.at[:, run, across],
            dst_ref=weights.at[:, run, across],
            send_sem=ag_z_send.at[j],
            recv_sem=ag_z_recv.at[j],
            device_id=run_peer(j),
            device_id_type=MESH,
        )
        copy.start()
        z_copies.append(copy)

    def fan_out(block):
        for j in range(1, wide):
            pltpu.make_async_remote_copy(
                src_ref=weights.at[:, block, across],
                dst_ref=weights.at[:, block, across],
                send_sem=ag_x_send,
                recv_sem=ag_x_recv,
                device_id=wide_peer(j),
                device_id_type=MESH,
            ).start()

    fan_out(run)

    x_rows = dot_tn(place[...], tok_ref[...])
    c_rows = dot_tn(place[...], cot_ref[...])
    cot_rows[...] = c_rows.astype(BF16)
    per_expert = sum(dot_tn(place[...], part) for part in parts_of(weight))
    slot_share = jnp.sum(jnp.where(slot_expert, per_expert, 0.0), axis=1, keepdims=True)
    row_share[...] = slot_share
    outbox[...] = paired(x_rows, slot_share * c_rows, experts)

    own_rows = pltpu.make_async_copy(outbox.at[me], inbox.at[0, my_member], self_sem.at[0])
    own_rows.start()

    def send_rows(step, first):
        def send(i, carry):
            peer, _ = expert_at(step, i)
            pltpu.make_async_remote_copy(
                src_ref=outbox.at[peer],
                dst_ref=inbox.at[(stretches - step) % stretches, my_member],
                send_sem=row_send,
                recv_sem=row_recv.at[(stretches - step) % stretches],
                device_id={"expert": peer},
                device_id_type=MESH,
            ).start()
            return carry

        lax.fori_loop(first, members, send, 0)

    far_first = sorted(range(1, stretches), key=lambda s: -min(s, stretches - s))
    for step in far_first:
        send_rows(step, 0)
    send_rows(0, 1)

    for j in range(1, runs):
        z_copies[j - 1].wait_recv()
        fan_out(lax.rem(run + runs - j, runs))
    blocks_in = weights.at[:, :, pl.ds(0, wide - 1)]
    pltpu.make_async_copy(blocks_in, blocks_in, ag_x_recv).wait()

    def wait_bytes(ref, sem):
        pltpu.make_async_copy(ref, ref, sem).wait()

    own_back = None
    for step in [0] + far_first[::-1]:
        if step == 0:
            own_rows.wait()
            wait_bytes(inbox.at[0, pl.ds(0, members - 1)], row_recv.at[0])
        else:
            wait_bytes(inbox.at[step], row_recv.at[step])
        rows = pl.ds(step * group_rows, group_rows)
        x_f32, g_f32 = unpaired(inbox[step])
        x = x_f32.astype(BF16)
        g = g_f32.astype(BF16)
        xs[rows] = x
        gs[rows] = g
        for column in range(0, hid, COLUMNS):
            columns = pl.ds(column, COLUMNS)
            active = jnp.maximum(dot(x, weights[0, :, :, :, columns].reshape(lat, COLUMNS)), 0.0)
            hidden_grad = dot(g, weights[1, :, :, :, columns].reshape(lat, COLUMNS))
            hs[rows, columns] = (active * active).astype(BF16)
            acts[rows, columns] = (2.0 * active * hidden_grad).astype(BF16)
        out = dot_nt(hs[rows], weights[1].reshape(lat, hid))
        row_grad = dot_nt(acts[rows], weights[0].reshape(lat, hid))
        reply[step] = paired(out, row_grad, members)

        if step == 0:
            own_back = pltpu.make_async_copy(
                reply.at[0, my_member], home.at[me], self_sem.at[1]
            )
            own_back.start()

        def send_back(i, carry, step=step):
            peer, member = expert_at(step, i)
            pltpu.make_async_remote_copy(
                src_ref=reply.at[step, member],
                dst_ref=home.at[me],
                send_sem=back_send,
                recv_sem=back_recv,
                device_id={"expert": peer},
                device_id_type=MESH,
            ).start()
            return carry

        lax.fori_loop(1 if step == 0 else 0, members, send_back, 0)

    for w, (left, right) in enumerate(((xs, acts), (gs, hs))):
        for column in range(0, hid, COLUMNS):
            columns = pl.ds(column, COLUMNS)
            term = dot_tn(left[...], right[:, columns])
            partial[w, :, :, :, columns] = term.reshape(runs, wide, -1, COLUMNS).astype(BF16)
        for j in range(1, wide):
            there = lax.rem(across + j, wide)
            pltpu.make_async_remote_copy(
                src_ref=partial.at[w, :, there],
                dst_ref=x_in.at[w, j - 1],
                send_sem=rs_x_send.at[w],
                recv_sem=rs_x_recv.at[w],
                device_id=wide_peer(j),
                device_id_type=MESH,
            ).start()
    for w in range(2):
        wait_bytes(x_in.at[w], rs_x_recv.at[w])
        total = partial[w, :, across].astype(F32)
        for j in range(wide - 1):
            total += x_in[w, j].astype(F32)
        z_out[w] = total.astype(BF16)
        for j in range(1, runs):
            pltpu.make_async_remote_copy(
                src_ref=z_out.at[w, lax.rem(run + j, runs)],
                dst_ref=z_in.at[w, j - 1],
                send_sem=rs_z_send.at[w],
                recv_sem=rs_z_recv.at[w],
                device_id=run_peer(j),
                device_id_type=MESH,
            ).start()
    for w, grad_ref in enumerate((up_grad_ref, down_grad_ref)):
        wait_bytes(z_in.at[w], rs_z_recv.at[w])
        total = z_out[w, run].astype(F32)
        for j in range(runs - 1):
            total += z_in[w, j].astype(F32)
        grad_ref[0] = total

    own_back.wait()
    wait_bytes(home.at[pl.ds(0, experts - 1)], back_recv)
    out, row_grad = unpaired(home[...])
    share = row_share[...]
    lat_ref[...] = dot(place[...], row_grad.astype(BF16)).astype(BF16)
    first, second, _ = parts_of(share * out)
    comb_ref[...] = (dot(place[...], first) + dot(place[...], second)).astype(BF16)
    row_prob = jnp.sum(cot_rows[...].astype(F32) * out, axis=1, keepdims=True)
    by_expert = sum(
        dot(place[...], part) for part in parts_of(jnp.where(slot_expert, row_prob, 0.0))
    )
    rank_lane = lax.broadcasted_iota(jnp.int32, (tokens, top), 1)
    prob = jnp.zeros((tokens, top), F32)
    for k in range(top):
        hit = picks[:, k : k + 1] == expert_lane
        value = jnp.sum(jnp.where(hit, by_expert, 0.0), axis=1, keepdims=True)
        prob = jnp.where(rank_lane == k, value, prob)
    prob_ref[...] = prob

    for copy in z_copies:
        copy.wait_send()
    wait_bytes(blocks_in, ag_x_send)
    wait_bytes(outbox.at[pl.ds(0, experts - 1)], row_send)
    wait_bytes(home.at[pl.ds(0, experts - 1)], back_send)
    for w in range(2):
        wait_bytes(x_in.at[w], rs_x_send.at[w])
        wait_bytes(z_in.at[w], rs_z_send.at[w])


def body(
    compressed_tokens,
    picked_specialists,
    gating_shares,
    seat_limits,
    raising_factors,
    lowering_factors,
    result_cotangent,
):
    runs, wide = DP_GRID
    ys, stretches, cores = EXPERT_GRID
    experts = ys * stretches * cores
    members = ys * cores
    tokens, lat = compressed_tokens.shape
    top = picked_specialists.shape[1]
    _, depth, hid = raising_factors.shape
    slots = experts * SEATS
    vmem = pl.BlockSpec(memory_space=pltpu.VMEM)
    dma = pltpu.SemaphoreType.DMA
    return pl.pallas_call(
        kernel,
        out_shape=(
            jax.ShapeDtypeStruct((tokens, lat), BF16),
            jax.ShapeDtypeStruct((tokens, lat), BF16),
            jax.ShapeDtypeStruct((tokens, top), F32),
            jax.ShapeDtypeStruct((1, depth, hid), F32),
            jax.ShapeDtypeStruct((1, depth, hid), F32),
        ),
        in_specs=[vmem] * 7,
        out_specs=[vmem] * 5,
        scratch_shapes=[
            pltpu.VMEM((2, runs, wide, depth, hid), BF16),
            pltpu.VMEM((experts, PAIR, lat), BF16),
            pltpu.VMEM((stretches, members, PAIR, lat), BF16),
            pltpu.VMEM((stretches, members, PAIR, lat), BF16),
            pltpu.VMEM((experts, PAIR, lat), BF16),
            pltpu.VMEM((tokens, slots), BF16),
            pltpu.VMEM((slots, lat), BF16),
            pltpu.VMEM((slots, 1), F32),
            pltpu.VMEM((slots, lat), BF16),
            pltpu.VMEM((slots, lat), BF16),
            pltpu.VMEM((slots, hid), BF16),
            pltpu.VMEM((slots, hid), BF16),
            pltpu.VMEM((2, runs, wide, depth, hid), BF16),
            pltpu.VMEM((2, wide - 1, runs, depth, hid), BF16),
            pltpu.VMEM((2, runs, depth, hid), BF16),
            pltpu.VMEM((2, runs - 1, depth, hid), BF16),
            dma((runs,)),
            dma((runs,)),
            dma,
            dma,
            dma,
            dma((stretches,)),
            dma,
            dma,
            dma((2,)),
            dma((2,)),
            dma((2,)),
            dma((2,)),
            dma((2,)),
        ],
        compiler_params=pltpu.CompilerParams(
            collective_id=0, has_side_effects=True, vmem_limit_bytes=48 * 1024 * 1024
        ),
        name="moe_layer",
    )(
        compressed_tokens,
        picked_specialists,
        gating_shares,
        seat_limits.reshape(1, -1),
        raising_factors,
        lowering_factors,
        result_cotangent,
    )


def solution(mesh):
    in_specs = (
        P(("dp", "expert"), None),
        P(("dp", "expert"), None),
        P(("dp", "expert"), None),
        P(),
        P("expert", "dp", None),
        P("expert", "dp", None),
        P(("dp", "expert"), None),
    )
    out_specs = (
        P(("dp", "expert"), None),
        P(("dp", "expert"), None),
        P(("dp", "expert"), None),
        P("expert", "dp", None),
        P("expert", "dp", None),
    )
    return jax.shard_map(body, mesh=mesh, in_specs=in_specs, out_specs=out_specs, check_vma=False)
```

```python
import functools

import jax
import jax.numpy as jnp
from jax import lax
from jax.experimental import pallas as pl
from jax.experimental.pallas import tpu as pltpu
from jax.sharding import PartitionSpec as P

DP_GRID = (4, 4)
EXPERT_GRID = (8, 4, 2)
SEATS = 8
ROOMS = (104, 112, 128)
PAIR = 2 * SEATS
COLUMNS = 256
CHUNKS = 2
MESH = pl.DeviceIdType.MESH
BF16 = jnp.bfloat16
F32 = jnp.float32


def dot(a, b):
    return jnp.dot(a, b, preferred_element_type=F32)


def dot_nt(a, b):
    return lax.dot_general(a, b, (((1,), (1,)), ((), ())), preferred_element_type=F32)


def dot_tn(a, b):
    return lax.dot_general(a, b, (((0,), (0,)), ((), ())), preferred_element_type=F32)


def parts_of(values):
    first = values.astype(BF16)
    rest = values - first.astype(F32)
    second = rest.astype(BF16)
    third = (rest - second.astype(F32)).astype(BF16)
    return first, second, third


def paired(upper, lower, blocks):
    width = upper.shape[-1]
    return jnp.concatenate(
        [upper.reshape(blocks, SEATS, width), lower.reshape(blocks, SEATS, width)], axis=1
    ).astype(BF16)


def unpaired(blocks):
    count, _, width = blocks.shape
    wide = blocks.astype(F32)
    return (
        wide[:, :SEATS].reshape(count * SEATS, width),
        wide[:, SEATS:].reshape(count * SEATS, width),
    )


def kernel(
    room,
    tok_hbm, cot_hbm, up_hbm, down_hbm, pick_hbm, share_hbm, limit_hbm,
    comb_ref, lat_ref, prob_ref, up_grad_ref, down_grad_ref,
    weights, tok, cot, pick_ref, share_ref, limit_ref, own_out, outbox, middle, inbox, reply, gather, packed, own_home, home,
    place, place_t, unfold, unfolded, cot_rows, row_share, xs, gs, hs, acts, partial, x_in, z_out, z_in,
    load_sem, ag_z_send, ag_z_recv, ag_x_send, ag_x_recv,
    out_z_send, out_z_recv, out_y_send, out_y_recv, out_self,
    back_y_send, back_y_recv, back_z_send, back_z_recv, back_self,
    rs_x_send, rs_x_recv, rs_z_send, rs_z_recv, turn_sem,
):
    runs, wide = DP_GRID
    ys, stretches, cores = EXPERT_GRID
    experts = ys * stretches * cores
    members = ys * cores
    tokens, lat = tok.shape
    top = pick_ref.shape[0]
    hid = weights.shape[-1]
    group_rows = members * SEATS
    near_slots = members * SEATS
    slots = place.shape[0]

    dp = lax.axis_index("dp")
    me = lax.axis_index("expert")
    run, across = dp // wide, dp % wide
    my_stretch = (me // cores) % stretches
    my_member = (me // (stretches * cores)) * cores + me % cores

    def run_peer(j):
        return {"dp": lax.rem(run + j, runs) * wide + across}

    def wide_peer(j):
        return {"dp": run * wide + lax.rem(across + j, wide)}

    def expert_of(stretch, member):
        return ((member // cores) * stretches + stretch) * cores + member % cores

    def member_peer(i):
        return {"expert": expert_of(my_stretch, lax.rem(my_member + i, members))}

    def stretch_peer(j):
        return {"expert": expert_of(lax.rem(my_stretch + j, stretches), my_member)}

    def steps_to(expert):
        member = expert // (stretches * cores) * cores + expert % cores
        return (
            (expert // cores + stretches - my_stretch) % stretches,
            (member + members - my_member) % members,
        )

    def remote(src, dst, send_sem, recv_sem, peer):
        return pltpu.make_async_remote_copy(
            src_ref=src, dst_ref=dst, send_sem=send_sem, recv_sem=recv_sem,
            device_id=peer, device_id_type=MESH,
        )

    def wait_bytes(ref, sem):
        pltpu.make_async_copy(ref, ref, sem).wait()

    loads = [
        pltpu.make_async_copy(src, dst, load_sem.at[i])
        for i, (src, dst) in enumerate(
            (
                (up_hbm.at[0], weights.at[0, run, across]),
                (down_hbm.at[0], weights.at[1, run, across]),
                (pick_hbm, pick_ref),
                (share_hbm, share_ref),
                (limit_hbm, limit_ref),
                (tok_hbm, tok),
                (cot_hbm, cot),
            )
        )
    ]
    for load in loads:
        load.start()

    barrier = pltpu.get_barrier_semaphore()
    peers = [run_peer(j) for j in range(1, runs)] + [wide_peer(j) for j in range(1, wide)]
    peers += [stretch_peer(j) for j in range(1, stretches)]
    for peer in peers:
        pl.semaphore_signal(barrier, inc=1, device_id=peer, device_id_type=MESH)

    def greet(i, carry):
        pl.semaphore_signal(barrier, inc=1, device_id=member_peer(i), device_id_type=MESH)
        return carry

    lax.fori_loop(1, members, greet, 0)

    for load in loads[2:5]:
        load.wait()

    picks = pick_ref[...]
    shares = share_ref[...]
    expert_row = lax.broadcasted_iota(jnp.int32, (experts, tokens), 0)
    named = jnp.zeros((experts, tokens), F32)
    weight = jnp.zeros((experts, tokens), F32)
    for k in range(top):
        hit = picks[k : k + 1] == expert_row
        named = jnp.where(hit, 1.0, named)
        weight = jnp.where(hit, shares[k : k + 1], weight)
    earlier = (
        lax.broadcasted_iota(jnp.int32, (tokens, tokens), 0)
        < lax.broadcasted_iota(jnp.int32, (tokens, tokens), 1)
    ).astype(BF16)
    position = dot(named.astype(BF16), earlier)
    square = lax.broadcasted_iota(jnp.int32, (experts, experts), 0) == lax.broadcasted_iota(
        jnp.int32, (experts, experts), 1
    )
    limit_row = limit_ref[...].astype(F32)
    limit = jnp.sum(jnp.where(square, limit_row, 0.0), axis=1, keepdims=True)
    seat = jnp.where((named > 0.0) & (position < limit), position, -1.0).astype(BF16)
    across_stretch, along_members = steps_to(lax.broadcasted_iota(jnp.int32, (1, experts), 1))
    down_stretch, down_members = steps_to(lax.broadcasted_iota(jnp.int32, (experts, 1), 0))
    ahead = (down_stretch == across_stretch) & (down_members < along_members)
    offset = jnp.sum(jnp.where(ahead, limit, 0.0), axis=0, keepdims=True)
    first_slot = jnp.where(
        across_stretch == 0,
        (along_members * SEATS).astype(F32),
        (near_slots + (across_stretch - 1) * room).astype(F32) + offset,
    )
    slot = lax.broadcasted_iota(jnp.int32, (slots, experts), 0).astype(F32)
    slot_expert = (slot >= first_slot) & (slot < first_slot + limit_row)
    taken = jnp.sum(jnp.where(slot_expert, 1.0, 0.0), axis=1, keepdims=True)
    slot_seat = jnp.sum(jnp.where(slot_expert, slot - first_slot, 0.0), axis=1, keepdims=True)
    slot_seat = jnp.where(taken > 0.0, slot_seat, -2.0)
    place[...] = (dot(slot_expert.astype(BF16), seat) == slot_seat).astype(BF16)
    row = lax.broadcasted_iota(jnp.int32, (members * PAIR, experts), 0)
    row_expert = (across_stretch == 0) & (along_members == row // PAIR)
    row_first = jnp.sum(jnp.where(row_expert, offset, 0.0), axis=1, keepdims=True)
    row_limit = jnp.sum(jnp.where(row_expert, limit_row, 0.0), axis=1, keepdims=True)
    row = lax.broadcasted_iota(jnp.int32, (members * PAIR, 1), 0)
    row_seat = (row % SEATS).astype(F32)
    row_source = jnp.where(
        row_seat < row_limit,
        ((row % PAIR) // SEATS * room).astype(F32) + row_first + row_seat,
        -1.0,
    )
    packed_row = lax.broadcasted_iota(jnp.int32, (members * PAIR, 2 * room), 1).astype(F32)
    unfold[...] = (packed_row == row_source).astype(BF16)

    loads[0].wait()
    loads[1].wait()
    pl.semaphore_wait(barrier, len(peers) + members - 1)

    z_copies = []
    own = weights.at[:, run, across]
    for j in range(1, runs):
        copy = remote(own, own, ag_z_send.at[j], ag_z_recv.at[j], run_peer(j))
        copy.start()
        z_copies.append(copy)

    def fan_out(block):
        for j in range(1, wide):
            part = weights.at[:, block, across]
            remote(part, part, ag_x_send, ag_x_recv, wide_peer(j)).start()

    fan_out(run)

    loads[5].wait()
    loads[6].wait()
    x_rows = dot(place[...], tok[...])
    c_rows = dot(place[...], cot[...])
    cot_rows[...] = c_rows.astype(BF16)
    per_expert = sum(dot_nt(place[...], part) for part in parts_of(weight))
    slot_share = jnp.sum(jnp.where(slot_expert, per_expert, 0.0), axis=1, keepdims=True)
    row_share[...] = slot_share
    g_rows = slot_share * c_rows
    own_out[...] = paired(x_rows[:near_slots], g_rows[:near_slots], members)
    for j in range(1, stretches):
        first = near_slots + (j - 1) * room
        outbox[j - 1] = jnp.concatenate(
            [x_rows[first : first + room], g_rows[first : first + room]], axis=0
        ).astype(BF16)

    def spread(source, there):
        pltpu.make_async_copy(source.at[0], inbox.at[there, 0], out_self.at[there]).start()

        def send(i, carry):
            remote(
                source.at[i], inbox.at[there, members - i],
                out_y_send, out_y_recv.at[there], member_peer(i),
            ).start()
            return carry

        lax.fori_loop(1, members, send, 0)

    spread(own_out, 0)

    for j in range(1, runs):
        z_copies[j - 1].wait_recv()
        fan_out(lax.rem(run + runs - j, runs))

    order = sorted(range(1, stretches), key=lambda j: min(j, stretches - j))
    near, far = order[:-1], order[-1]

    def set_out(j):
        remote(
            outbox.at[j - 1], middle.at[j - 1], out_z_send, out_z_recv.at[j], stretch_peer(j)
        ).start()

    def tell_run(turn):
        for j in range(1, runs):
            pl.semaphore_signal(
                turn_sem.at[turn], inc=1, device_id=run_peer(j), device_id_type=MESH
            )

    def wait_run(turn):
        pl.semaphore_wait(turn_sem.at[turn], runs - 1)

    tell_run(0)
    wait_run(0)
    for j in near:
        set_out(j)

    def arrive(j):
        wait_bytes(middle.at[j - 1], out_z_recv.at[j])

    def forward(j):
        blocks = dot(unfold[...], middle[j - 1]).astype(BF16)
        unfolded[j - 1] = blocks.reshape(unfolded.shape[1:])
        spread(unfolded.at[j - 1], (stretches - j) % stretches)

    def expert_step(there):
        pltpu.make_async_copy(inbox.at[there, 0], inbox.at[there, 0], out_self.at[there]).wait()
        wait_bytes(inbox.at[there, pl.ds(1, members - 1)], out_y_recv.at[there])
        rows = pl.ds(there * group_rows, group_rows)
        x_f32, g_f32 = unpaired(inbox[there])
        x = x_f32.astype(BF16)
        g = g_f32.astype(BF16)
        xs[rows] = x
        gs[rows] = g
        for column in range(0, hid, COLUMNS):
            columns = pl.ds(column, COLUMNS)
            active = jnp.maximum(dot(x, weights[0, :, :, :, columns].reshape(lat, COLUMNS)), 0.0)
            hidden_grad = dot(g, weights[1, :, :, :, columns].reshape(lat, COLUMNS))
            hs[rows, columns] = (active * active).astype(BF16)
            acts[rows, columns] = (2.0 * active * hidden_grad).astype(BF16)
        out = dot_nt(hs[rows], weights[1].reshape(lat, hid))
        row_grad = dot_nt(acts[rows], weights[0].reshape(lat, hid))
        reply[there] = paired(out, row_grad, members)
        target = own_home if there == 0 else gather.at[there - 1]
        pltpu.make_async_copy(reply.at[there, 0], target.at[0], back_self.at[there]).start()

        def send(i, carry):
            remote(
                reply.at[there, i], target.at[members - i],
                back_y_send, back_y_recv.at[there], member_peer(i),
            ).start()
            return carry

        lax.fori_loop(1, members, send, 0)

    def gathered(there):
        target = own_home if there == 0 else gather.at[there - 1]
        pltpu.make_async_copy(target.at[0], target.at[0], back_self.at[there]).wait()
        wait_bytes(target.at[pl.ds(1, members - 1)], back_y_recv.at[there])

    def go_home(there):
        gathered(there)
        rows = gather[there - 1].reshape(members * PAIR, lat)
        packed[there - 1] = dot_tn(unfold[...], rows).astype(BF16)
        j = stretches - there
        remote(
            packed.at[there - 1], home.at[j - 1],
            back_z_send, back_z_recv.at[j], stretch_peer(there),
        ).start()

    for j in near:
        arrive(j)
    tell_run(1)
    for j in near:
        forward(j)
    wait_run(1)
    set_out(far)
    place_t[...] = place[...].T
    blocks_in = weights.at[:, :, pl.ds(0, wide - 1)]
    wait_bytes(blocks_in, ag_x_recv)
    expert_step(0)
    for j in near:
        expert_step(stretches - j)
    arrive(far)
    forward(far)
    for j in near:
        go_home(stretches - j)
    expert_step(stretches - far)

    chunk_columns = hid // CHUNKS
    chunks = [
        (grad_ref, left, right, half * chunk_columns)
        for grad_ref, left, right in ((up_grad_ref, xs, acts), (down_grad_ref, gs, hs))
        for half in range(CHUNKS)
    ]
    for q, (_, left, right, start) in enumerate(chunks):
        for column in range(0, chunk_columns, COLUMNS):
            term = dot_tn(left[...], right[:, pl.ds(start + column, COLUMNS)])
            term = term.reshape(runs, wide, -1, COLUMNS).astype(BF16)
            partial[q, :, :, :, pl.ds(column, COLUMNS)] = term
        for j in range(1, wide):
            there = lax.rem(across + j, wide)
            remote(
                partial.at[q, :, there], x_in.at[q, j - 1],
                rs_x_send.at[q], rs_x_recv.at[q], wide_peer(j),
            ).start()
    for q in range(len(chunks)):
        wait_bytes(x_in.at[q], rs_x_recv.at[q])
        total = partial[q, :, across].astype(F32)
        for j in range(wide - 1):
            total += x_in[q, j].astype(F32)
        z_out[q] = total.astype(BF16)
        for j in range(1, runs):
            remote(
                z_out.at[q, lax.rem(run + j, runs)], z_in.at[q, j - 1],
                rs_z_send.at[q], rs_z_recv.at[q], run_peer(j),
            ).start()
        if q == 0:
            go_home(stretches - far)
    for q, (grad_ref, _, _, start) in enumerate(chunks):
        wait_bytes(z_in.at[q], rs_z_recv.at[q])
        total = z_out[q, run].astype(F32)
        for j in range(runs - 1):
            total += z_in[q, j].astype(F32)
        grad_ref[0, :, pl.ds(start, chunk_columns)] = total

    gathered(0)
    for j in range(1, stretches):
        wait_bytes(home.at[j - 1], back_z_recv.at[j])
    outs, row_grads = ([rows] for rows in unpaired(own_home[...]))
    for j in range(1, stretches):
        rows = home[j - 1].astype(F32)
        outs.append(rows[:room])
        row_grads.append(rows[room:])
    spare = slots - near_slots - (stretches - 1) * room
    if spare:
        outs.append(jnp.zeros((spare, lat), F32))
        row_grads.append(jnp.zeros((spare, lat), F32))
    out = jnp.concatenate(outs, axis=0)
    row_grad = jnp.concatenate(row_grads, axis=0)
    lat_ref[...] = dot(place_t[...], row_grad.astype(BF16)).astype(BF16)
    first, second, _ = parts_of(row_share[...] * out)
    comb_ref[...] = (dot(place_t[...], first) + dot(place_t[...], second)).astype(BF16)
    row_prob = jnp.sum(cot_rows[...].astype(F32) * out, axis=1, keepdims=True)
    by_expert = sum(
        dot_tn(part, place[...]) for part in parts_of(jnp.where(slot_expert, row_prob, 0.0))
    )
    for k in range(top):
        hit = picks[k : k + 1] == expert_row
        prob_ref[k : k + 1] = jnp.sum(jnp.where(hit, by_expert, 0.0), axis=0, keepdims=True)

    for copy in z_copies:
        copy.wait_send()
    wait_bytes(blocks_in, ag_x_send)
    wait_bytes(outbox, out_z_send)
    wait_bytes(inbox.at[:, pl.ds(1, members - 1)], out_y_send)
    wait_bytes(inbox.at[:, pl.ds(1, members - 1)], back_y_send)
    wait_bytes(home, back_z_send)
    for q in range(len(chunks)):
        wait_bytes(x_in.at[q], rs_x_send.at[q])
        wait_bytes(z_in.at[q], rs_z_send.at[q])


def layer(
    room,
    kernel_id,
    compressed_tokens,
    picked_specialists,
    gating_shares,
    seat_limits,
    raising_factors,
    lowering_factors,
    result_cotangent,
):
    runs, wide = DP_GRID
    ys, stretches, cores = EXPERT_GRID
    experts = ys * stretches * cores
    members = ys * cores
    tokens, lat = compressed_tokens.shape
    top = picked_specialists.shape[0]
    _, depth, hid = raising_factors.shape
    near_slots = members * SEATS
    slots = -(-(near_slots + (stretches - 1) * room) // 128) * 128
    rows = experts * SEATS
    vmem = pl.BlockSpec(memory_space=pltpu.VMEM)
    hbm = pl.BlockSpec(memory_space=pltpu.HBM)
    dma = pltpu.SemaphoreType.DMA
    blocks = pltpu.VMEM((stretches, members, PAIR, lat), BF16)
    far_blocks = pltpu.VMEM((stretches - 1, members, PAIR, lat), BF16)
    own_blocks = pltpu.VMEM((members, PAIR, lat), BF16)
    folded = pltpu.VMEM((stretches - 1, 2 * room, lat), BF16)
    outs = (
        jax.ShapeDtypeStruct((tokens, lat), BF16),
        jax.ShapeDtypeStruct((tokens, lat), BF16),
        jax.ShapeDtypeStruct((top, tokens), F32),
        jax.ShapeDtypeStruct((1, depth, hid), F32),
        jax.ShapeDtypeStruct((1, depth, hid), F32),
    )
    return pl.pallas_call(
        functools.partial(kernel, room),
        out_shape=outs,
        in_specs=[hbm] * 7,
        out_specs=[vmem] * 5,
        scratch_shapes=[
            pltpu.VMEM((2, runs, wide, depth, hid), BF16),
            pltpu.VMEM((tokens, lat), BF16),
            pltpu.VMEM((tokens, lat), BF16),
            pltpu.VMEM((top, tokens), jnp.int32),
            pltpu.VMEM((top, tokens), F32),
            pltpu.VMEM((1, experts), jnp.int32),
            own_blocks,
            folded,
            folded,
            blocks,
            blocks,
            far_blocks,
            folded,
            own_blocks,
            folded,
            pltpu.VMEM((slots, tokens), BF16),
            pltpu.VMEM((tokens, slots), BF16),
            pltpu.VMEM((members * PAIR, 2 * room), BF16),
            far_blocks,
            pltpu.VMEM((slots, lat), BF16),
            pltpu.VMEM((slots, 1), F32),
            pltpu.VMEM((rows, lat), BF16),
            pltpu.VMEM((rows, lat), BF16),
            pltpu.VMEM((rows, hid), BF16),
            pltpu.VMEM((rows, hid), BF16),
            pltpu.VMEM((2 * CHUNKS, runs, wide, depth, hid // CHUNKS), BF16),
            pltpu.VMEM((2 * CHUNKS, wide - 1, runs, depth, hid // CHUNKS), BF16),
            pltpu.VMEM((2 * CHUNKS, runs, depth, hid // CHUNKS), BF16),
            pltpu.VMEM((2 * CHUNKS, runs - 1, depth, hid // CHUNKS), BF16),
            dma((7,)),
            dma((runs,)),
            dma((runs,)),
            dma,
            dma,
            dma,
            dma((stretches,)),
            dma,
            dma((stretches,)),
            dma((stretches,)),
            dma,
            dma((stretches,)),
            dma,
            dma((stretches,)),
            dma((stretches,)),
            dma((2 * CHUNKS,)),
            dma((2 * CHUNKS,)),
            dma((2 * CHUNKS,)),
            dma((2 * CHUNKS,)),
            pltpu.SemaphoreType.REGULAR((2,)),
        ],
        compiler_params=pltpu.CompilerParams(
            collective_id=kernel_id, has_side_effects=True, vmem_limit_bytes=60 * 1024 * 1024
        ),
        name="moe_layer",
    )(
        compressed_tokens,
        result_cotangent,
        raising_factors,
        lowering_factors,
        picked_specialists,
        gating_shares,
        seat_limits,
    )


def body(
    compressed_tokens,
    picked_specialists,
    gating_shares,
    seat_limits,
    raising_factors,
    lowering_factors,
    result_cotangent,
):
    ys, stretches, cores = EXPERT_GRID
    most = jnp.max(jnp.sum(seat_limits.reshape(ys, stretches, cores), axis=(0, 2)))
    choice = sum((most > room).astype(jnp.int32) for room in ROOMS[:-1])
    combined, latent_grad, prob_grad, up_grad, down_grad = lax.switch(
        choice,
        [functools.partial(layer, room, i) for i, room in enumerate(ROOMS)],
        compressed_tokens,
        picked_specialists.T,
        gating_shares.T,
        seat_limits.reshape(1, -1),
        raising_factors,
        lowering_factors,
        result_cotangent,
    )
    return combined, latent_grad, prob_grad.T, up_grad, down_grad


def solution(mesh):
    in_specs = (
        P(("dp", "expert"), None),
        P(("dp", "expert"), None),
        P(("dp", "expert"), None),
        P(),
        P("expert", "dp", None),
        P("expert", "dp", None),
        P(("dp", "expert"), None),
    )
    out_specs = (
        P(("dp", "expert"), None),
        P(("dp", "expert"), None),
        P(("dp", "expert"), None),
        P("expert", "dp", None),
        P("expert", "dp", None),
    )
    return jax.shard_map(body, mesh=mesh, in_specs=in_specs, out_specs=out_specs, check_vma=False)
```

```python
import functools

import jax
import jax.numpy as jnp
from jax import lax
from jax.experimental import pallas as pl
from jax.experimental.pallas import tpu as pltpu
from jax.sharding import PartitionSpec as P

DP_GRID = (4, 4)
EXPERT_GRID = (8, 4, 2)
SEATS = 8
ROOMS = (104, 112, 128)
PAIR = 2 * SEATS
COLUMNS = 256
CHUNKS = 2
MESH = pl.DeviceIdType.MESH
BF16 = jnp.bfloat16
F32 = jnp.float32


def dot(a, b):
    return jnp.dot(a, b, preferred_element_type=F32)


def dot_nt(a, b):
    return lax.dot_general(a, b, (((1,), (1,)), ((), ())), preferred_element_type=F32)


def dot_tn(a, b):
    return lax.dot_general(a, b, (((0,), (0,)), ((), ())), preferred_element_type=F32)


def parts_of(values):
    first = values.astype(BF16)
    rest = values - first.astype(F32)
    second = rest.astype(BF16)
    third = (rest - second.astype(F32)).astype(BF16)
    return first, second, third


def paired(upper, lower, blocks):
    width = upper.shape[-1]
    return jnp.concatenate(
        [upper.reshape(blocks, SEATS, width), lower.reshape(blocks, SEATS, width)], axis=1
    ).astype(BF16)


def unpaired(blocks):
    count, _, width = blocks.shape
    wide = blocks.astype(F32)
    return (
        wide[:, :SEATS].reshape(count * SEATS, width),
        wide[:, SEATS:].reshape(count * SEATS, width),
    )


def kernel(
    room,
    tok_hbm, cot_hbm, up_hbm, down_hbm, pick_hbm, share_hbm, limit_hbm,
    comb_ref, lat_ref, prob_ref, up_grad_ref, down_grad_ref,
    weights, tok, cot, pick_ref, share_ref, limit_ref, own_out, outbox, middle, inbox, reply, gather, packed, own_home, home,
    place, place_t, unfold, unfolded, cot_rows, row_share, xs, gs, hs, acts, partial, x_in, z_out, z_in,
    load_sem, ag_z_send, ag_z_recv, ag_x_send, ag_x_recv,
    out_z_send, out_z_recv, out_y_send, out_y_recv, out_self,
    back_y_send, back_y_recv, back_z_send, back_z_recv, back_self,
    rs_x_send, rs_x_recv, rs_z_send, rs_z_recv,
):
    runs, wide = DP_GRID
    ys, stretches, cores = EXPERT_GRID
    experts = ys * stretches * cores
    members = ys * cores
    tokens, lat = tok.shape
    top = pick_ref.shape[0]
    hid = weights.shape[-1]
    group_rows = members * SEATS
    near_slots = members * SEATS
    slots = place.shape[0]

    dp = lax.axis_index("dp")
    me = lax.axis_index("expert")
    run, across = dp // wide, dp % wide
    my_stretch = (me // cores) % stretches
    my_member = (me // (stretches * cores)) * cores + me % cores

    def run_peer(j):
        return {"dp": lax.rem(run + j, runs) * wide + across}

    def wide_peer(j):
        return {"dp": run * wide + lax.rem(across + j, wide)}

    def expert_of(stretch, member):
        return ((member // cores) * stretches + stretch) * cores + member % cores

    def member_peer(i):
        return {"expert": expert_of(my_stretch, lax.rem(my_member + i, members))}

    def stretch_peer(j):
        return {"expert": expert_of(lax.rem(my_stretch + j, stretches), my_member)}

    def steps_to(expert):
        member = expert // (stretches * cores) * cores + expert % cores
        return (
            (expert // cores + stretches - my_stretch) % stretches,
            (member + members - my_member) % members,
        )

    def remote(src, dst, send_sem, recv_sem, peer):
        return pltpu.make_async_remote_copy(
            src_ref=src, dst_ref=dst, send_sem=send_sem, recv_sem=recv_sem,
            device_id=peer, device_id_type=MESH,
        )

    def wait_bytes(ref, sem):
        pltpu.make_async_copy(ref, ref, sem).wait()

    loads = [
        pltpu.make_async_copy(src, dst, load_sem.at[i])
        for i, (src, dst) in enumerate(
            (
                (up_hbm.at[0], weights.at[0, run, across]),
                (down_hbm.at[0], weights.at[1, run, across]),
                (pick_hbm, pick_ref),
                (share_hbm, share_ref),
                (limit_hbm, limit_ref),
                (tok_hbm, tok),
                (cot_hbm, cot),
            )
        )
    ]
    for load in loads:
        load.start()

    barrier = pltpu.get_barrier_semaphore()
    peers = [run_peer(j) for j in range(1, runs)] + [wide_peer(j) for j in range(1, wide)]
    peers += [stretch_peer(j) for j in range(1, stretches)]
    for peer in peers:
        pl.semaphore_signal(barrier, inc=1, device_id=peer, device_id_type=MESH)

    def greet(i, carry):
        pl.semaphore_signal(barrier, inc=1, device_id=member_peer(i), device_id_type=MESH)
        return carry

    lax.fori_loop(1, members, greet, 0)

    for load in loads[2:5]:
        load.wait()

    picks = pick_ref[...]
    shares = share_ref[...]
    expert_row = lax.broadcasted_iota(jnp.int32, (experts, tokens), 0)
    named = jnp.zeros((experts, tokens), F32)
    weight = jnp.zeros((experts, tokens), F32)
    for k in range(top):
        hit = picks[k : k + 1] == expert_row
        named = jnp.where(hit, 1.0, named)
        weight = jnp.where(hit, shares[k : k + 1], weight)
    earlier = (
        lax.broadcasted_iota(jnp.int32, (tokens, tokens), 0)
        < lax.broadcasted_iota(jnp.int32, (tokens, tokens), 1)
    ).astype(BF16)
    position = dot(named.astype(BF16), earlier)
    square = lax.broadcasted_iota(jnp.int32, (experts, experts), 0) == lax.broadcasted_iota(
        jnp.int32, (experts, experts), 1
    )
    limit_row = limit_ref[...].astype(F32)
    limit = jnp.sum(jnp.where(square, limit_row, 0.0), axis=1, keepdims=True)
    seat = jnp.where((named > 0.0) & (position < limit), position, -1.0).astype(BF16)
    across_stretch, along_members = steps_to(lax.broadcasted_iota(jnp.int32, (1, experts), 1))
    down_stretch, down_members = steps_to(lax.broadcasted_iota(jnp.int32, (experts, 1), 0))
    ahead = (down_stretch == across_stretch) & (down_members < along_members)
    offset = jnp.sum(jnp.where(ahead, limit, 0.0), axis=0, keepdims=True)
    first_slot = jnp.where(
        across_stretch == 0,
        (along_members * SEATS).astype(F32),
        (near_slots + (across_stretch - 1) * room).astype(F32) + offset,
    )
    slot = lax.broadcasted_iota(jnp.int32, (slots, experts), 0).astype(F32)
    slot_expert = (slot >= first_slot) & (slot < first_slot + limit_row)
    taken = jnp.sum(jnp.where(slot_expert, 1.0, 0.0), axis=1, keepdims=True)
    slot_seat = jnp.sum(jnp.where(slot_expert, slot - first_slot, 0.0), axis=1, keepdims=True)
    slot_seat = jnp.where(taken > 0.0, slot_seat, -2.0)
    place[...] = (dot(slot_expert.astype(BF16), seat) == slot_seat).astype(BF16)
    row = lax.broadcasted_iota(jnp.int32, (members * PAIR, experts), 0)
    row_expert = (across_stretch == 0) & (along_members == row // PAIR)
    row_first = jnp.sum(jnp.where(row_expert, offset, 0.0), axis=1, keepdims=True)
    row_limit = jnp.sum(jnp.where(row_expert, limit_row, 0.0), axis=1, keepdims=True)
    row = lax.broadcasted_iota(jnp.int32, (members * PAIR, 1), 0)
    row_seat = (row % SEATS).astype(F32)
    row_source = jnp.where(
        row_seat < row_limit,
        ((row % PAIR) // SEATS * room).astype(F32) + row_first + row_seat,
        -1.0,
    )
    packed_row = lax.broadcasted_iota(jnp.int32, (members * PAIR, 2 * room), 1).astype(F32)
    unfold[...] = (packed_row == row_source).astype(BF16)

    loads[0].wait()
    loads[1].wait()
    pl.semaphore_wait(barrier, len(peers) + members - 1)

    z_copies = [
        [
            remote(
                weights.at[w, run, across], weights.at[w, run, across],
                ag_z_send.at[w, j], ag_z_recv.at[w, j], run_peer(j),
            )
            for j in range(1, runs)
        ]
        for w in range(2)
    ]

    def fan_out(w, block):
        for j in range(1, wide):
            part = weights.at[w, block, across]
            remote(part, part, ag_x_send.at[w], ag_x_recv.at[w], wide_peer(j)).start()

    def pass_on(w):
        for j in range(1, runs):
            z_copies[w][j - 1].wait_recv()
            fan_out(w, lax.rem(run + runs - j, runs))

    for copy in z_copies[0]:
        copy.start()
    for w in range(2):
        fan_out(w, run)

    loads[5].wait()
    loads[6].wait()
    x_rows = dot(place[...], tok[...])
    c_rows = dot(place[...], cot[...])
    cot_rows[...] = c_rows.astype(BF16)
    per_expert = sum(dot_nt(place[...], part) for part in parts_of(weight))
    slot_share = jnp.sum(jnp.where(slot_expert, per_expert, 0.0), axis=1, keepdims=True)
    row_share[...] = slot_share
    g_rows = slot_share * c_rows
    own_out[...] = paired(x_rows[:near_slots], g_rows[:near_slots], members)
    for j in range(1, stretches):
        first = near_slots + (j - 1) * room
        outbox[j - 1] = jnp.concatenate(
            [x_rows[first : first + room], g_rows[first : first + room]], axis=0
        ).astype(BF16)

    def spread(source, there):
        pltpu.make_async_copy(source.at[0], inbox.at[there, 0], out_self.at[there]).start()

        def send(i, carry):
            remote(
                source.at[i], inbox.at[there, members - i],
                out_y_send, out_y_recv.at[there], member_peer(i),
            ).start()
            return carry

        lax.fori_loop(1, members, send, 0)

    order = sorted(range(1, stretches), key=lambda j: min(j, stretches - j))
    near, far = order[:-1], order[-1]

    def set_out(j):
        remote(
            outbox.at[j - 1], middle.at[j - 1], out_z_send, out_z_recv.at[j], stretch_peer(j)
        ).start()

    for j in near:
        set_out(j)
    spread(own_out, 0)
    pass_on(0)
    for copy in z_copies[1]:
        copy.start()

    def arrive(j):
        wait_bytes(middle.at[j - 1], out_z_recv.at[j])

    def forward(j):
        blocks = dot(unfold[...], middle[j - 1]).astype(BF16)
        unfolded[j - 1] = blocks.reshape(unfolded.shape[1:])
        spread(unfolded.at[j - 1], (stretches - j) % stretches)

    def expert_step(there):
        pltpu.make_async_copy(inbox.at[there, 0], inbox.at[there, 0], out_self.at[there]).wait()
        wait_bytes(inbox.at[there, pl.ds(1, members - 1)], out_y_recv.at[there])
        rows = pl.ds(there * group_rows, group_rows)
        x_f32, g_f32 = unpaired(inbox[there])
        x = x_f32.astype(BF16)
        g = g_f32.astype(BF16)
        xs[rows] = x
        gs[rows] = g
        for column in range(0, hid, COLUMNS):
            columns = pl.ds(column, COLUMNS)
            active = jnp.maximum(dot(x, weights[0, :, :, :, columns].reshape(lat, COLUMNS)), 0.0)
            hidden_grad = dot(g, weights[1, :, :, :, columns].reshape(lat, COLUMNS))
            hs[rows, columns] = (active * active).astype(BF16)
            acts[rows, columns] = (2.0 * active * hidden_grad).astype(BF16)
        out = dot_nt(hs[rows], weights[1].reshape(lat, hid))
        row_grad = dot_nt(acts[rows], weights[0].reshape(lat, hid))
        reply[there] = paired(out, row_grad, members)

    def send_back(there):
        target = own_home if there == 0 else gather.at[there - 1]
        pltpu.make_async_copy(reply.at[there, 0], target.at[0], back_self.at[there]).start()

        def send(i, carry):
            remote(
                reply.at[there, i], target.at[members - i],
                back_y_send, back_y_recv.at[there], member_peer(i),
            ).start()
            return carry

        lax.fori_loop(1, members, send, 0)

    def gathered(there):
        target = own_home if there == 0 else gather.at[there - 1]
        pltpu.make_async_copy(target.at[0], target.at[0], back_self.at[there]).wait()
        wait_bytes(target.at[pl.ds(1, members - 1)], back_y_recv.at[there])

    def go_home(there):
        gathered(there)
        rows = gather[there - 1].reshape(members * PAIR, lat)
        packed[there - 1] = dot_tn(unfold[...], rows).astype(BF16)
        j = stretches - there
        remote(
            packed.at[there - 1], home.at[j - 1],
            back_z_send, back_z_recv.at[j], stretch_peer(there),
        ).start()

    for j in near:
        arrive(j)
        forward(j)
    pass_on(1)
    set_out(far)
    place_t[...] = place[...].T
    for w in range(2):
        wait_bytes(weights.at[w, :, pl.ds(0, wide - 1)], ag_x_recv.at[w])
    for j in near:
        expert_step(stretches - j)
        send_back(stretches - j)
    expert_step(0)
    arrive(far)
    forward(far)
    for j in near:
        go_home(stretches - j)
    expert_step(stretches - far)
    send_back(stretches - far)
    send_back(0)

    chunk_columns = hid // CHUNKS
    chunks = [
        (grad_ref, left, right, half * chunk_columns)
        for grad_ref, left, right in ((up_grad_ref, xs, acts), (down_grad_ref, gs, hs))
        for half in range(CHUNKS)
    ]
    for q, (_, left, right, start) in enumerate(chunks):
        for column in range(0, chunk_columns, COLUMNS):
            term = dot_tn(left[...], right[:, pl.ds(start + column, COLUMNS)])
            term = term.reshape(runs, wide, -1, COLUMNS).astype(BF16)
            partial[q, :, :, :, pl.ds(column, COLUMNS)] = term
        for j in range(1, wide):
            there = lax.rem(across + j, wide)
            remote(
                partial.at[q, :, there], x_in.at[q, j - 1],
                rs_x_send.at[q], rs_x_recv.at[q], wide_peer(j),
            ).start()
    go_home(stretches - far)
    for q in range(len(chunks)):
        wait_bytes(x_in.at[q], rs_x_recv.at[q])
        total = partial[q, :, across].astype(F32)
        for j in range(wide - 1):
            total += x_in[q, j].astype(F32)
        z_out[q] = total.astype(BF16)
        for j in range(1, runs):
            remote(
                z_out.at[q, lax.rem(run + j, runs)], z_in.at[q, j - 1],
                rs_z_send.at[q], rs_z_recv.at[q], run_peer(j),
            ).start()
    for q, (grad_ref, _, _, start) in enumerate(chunks):
        wait_bytes(z_in.at[q], rs_z_recv.at[q])
        total = z_out[q, run].astype(F32)
        for j in range(runs - 1):
            total += z_in[q, j].astype(F32)
        grad_ref[0, :, pl.ds(start, chunk_columns)] = total

    gathered(0)
    for j in range(1, stretches):
        wait_bytes(home.at[j - 1], back_z_recv.at[j])
    outs, row_grads = ([rows] for rows in unpaired(own_home[...]))
    for j in range(1, stretches):
        rows = home[j - 1].astype(F32)
        outs.append(rows[:room])
        row_grads.append(rows[room:])
    spare = slots - near_slots - (stretches - 1) * room
    if spare:
        outs.append(jnp.zeros((spare, lat), F32))
        row_grads.append(jnp.zeros((spare, lat), F32))
    out = jnp.concatenate(outs, axis=0)
    row_grad = jnp.concatenate(row_grads, axis=0)
    lat_ref[...] = dot(place_t[...], row_grad.astype(BF16)).astype(BF16)
    first, second, _ = parts_of(row_share[...] * out)
    comb_ref[...] = (dot(place_t[...], first) + dot(place_t[...], second)).astype(BF16)
    row_prob = jnp.sum(cot_rows[...].astype(F32) * out, axis=1, keepdims=True)
    by_expert = sum(
        dot_tn(part, place[...]) for part in parts_of(jnp.where(slot_expert, row_prob, 0.0))
    )
    for k in range(top):
        hit = picks[k : k + 1] == expert_row
        prob_ref[k : k + 1] = jnp.sum(jnp.where(hit, by_expert, 0.0), axis=0, keepdims=True)

    for w in range(2):
        for copy in z_copies[w]:
            copy.wait_send()
        wait_bytes(weights.at[w, :, pl.ds(0, wide - 1)], ag_x_send.at[w])
    wait_bytes(outbox, out_z_send)
    wait_bytes(inbox.at[:, pl.ds(1, members - 1)], out_y_send)
    wait_bytes(inbox.at[:, pl.ds(1, members - 1)], back_y_send)
    wait_bytes(home, back_z_send)
    for q in range(len(chunks)):
        wait_bytes(x_in.at[q], rs_x_send.at[q])
        wait_bytes(z_in.at[q], rs_z_send.at[q])


def layer(
    room,
    kernel_id,
    compressed_tokens,
    picked_specialists,
    gating_shares,
    seat_limits,
    raising_factors,
    lowering_factors,
    result_cotangent,
):
    runs, wide = DP_GRID
    ys, stretches, cores = EXPERT_GRID
    experts = ys * stretches * cores
    members = ys * cores
    tokens, lat = compressed_tokens.shape
    top = picked_specialists.shape[0]
    _, depth, hid = raising_factors.shape
    near_slots = members * SEATS
    slots = -(-(near_slots + (stretches - 1) * room) // 128) * 128
    rows = experts * SEATS
    vmem = pl.BlockSpec(memory_space=pltpu.VMEM)
    hbm = pl.BlockSpec(memory_space=pltpu.HBM)
    dma = pltpu.SemaphoreType.DMA
    blocks = pltpu.VMEM((stretches, members, PAIR, lat), BF16)
    far_blocks = pltpu.VMEM((stretches - 1, members, PAIR, lat), BF16)
    own_blocks = pltpu.VMEM((members, PAIR, lat), BF16)
    folded = pltpu.VMEM((stretches - 1, 2 * room, lat), BF16)
    outs = (
        jax.ShapeDtypeStruct((tokens, lat), BF16),
        jax.ShapeDtypeStruct((tokens, lat), BF16),
        jax.ShapeDtypeStruct((top, tokens), F32),
        jax.ShapeDtypeStruct((1, depth, hid), F32),
        jax.ShapeDtypeStruct((1, depth, hid), F32),
    )
    return pl.pallas_call(
        functools.partial(kernel, room),
        out_shape=outs,
        in_specs=[hbm] * 7,
        out_specs=[vmem] * 5,
        scratch_shapes=[
            pltpu.VMEM((2, runs, wide, depth, hid), BF16),
            pltpu.VMEM((tokens, lat), BF16),
            pltpu.VMEM((tokens, lat), BF16),
            pltpu.VMEM((top, tokens), jnp.int32),
            pltpu.VMEM((top, tokens), F32),
            pltpu.VMEM((1, experts), jnp.int32),
            own_blocks,
            folded,
            folded,
            blocks,
            blocks,
            far_blocks,
            folded,
            own_blocks,
            folded,
            pltpu.VMEM((slots, tokens), BF16),
            pltpu.VMEM((tokens, slots), BF16),
            pltpu.VMEM((members * PAIR, 2 * room), BF16),
            far_blocks,
            pltpu.VMEM((slots, lat), BF16),
            pltpu.VMEM((slots, 1), F32),
            pltpu.VMEM((rows, lat), BF16),
            pltpu.VMEM((rows, lat), BF16),
            pltpu.VMEM((rows, hid), BF16),
            pltpu.VMEM((rows, hid), BF16),
            pltpu.VMEM((2 * CHUNKS, runs, wide, depth, hid // CHUNKS), BF16),
            pltpu.VMEM((2 * CHUNKS, wide - 1, runs, depth, hid // CHUNKS), BF16),
            pltpu.VMEM((2 * CHUNKS, runs, depth, hid // CHUNKS), BF16),
            pltpu.VMEM((2 * CHUNKS, runs - 1, depth, hid // CHUNKS), BF16),
            dma((7,)),
            dma((2, runs)),
            dma((2, runs)),
            dma((2,)),
            dma((2,)),
            dma,
            dma((stretches,)),
            dma,
            dma((stretches,)),
            dma((stretches,)),
            dma,
            dma((stretches,)),
            dma,
            dma((stretches,)),
            dma((stretches,)),
            dma((2 * CHUNKS,)),
            dma((2 * CHUNKS,)),
            dma((2 * CHUNKS,)),
            dma((2 * CHUNKS,)),
        ],
        compiler_params=pltpu.CompilerParams(
            collective_id=kernel_id, has_side_effects=True, vmem_limit_bytes=60 * 1024 * 1024
        ),
        name="moe_layer",
    )(
        compressed_tokens,
        result_cotangent,
        raising_factors,
        lowering_factors,
        picked_specialists,
        gating_shares,
        seat_limits,
    )


def store_kernel(*refs):
    count = len(refs) // 2
    for src, dst in zip(refs[:count], refs[count:]):
        dst[...] = src[...]


def body(
    compressed_tokens,
    picked_specialists,
    gating_shares,
    seat_limits,
    raising_factors,
    lowering_factors,
    result_cotangent,
):
    ys, stretches, cores = EXPERT_GRID
    most = jnp.max(jnp.sum(seat_limits.reshape(ys, stretches, cores), axis=(0, 2)))
    choice = sum((most > room).astype(jnp.int32) for room in ROOMS[:-1])
    combined, latent_grad, prob_grad, up_grad, down_grad = lax.switch(
        choice,
        [functools.partial(layer, room, i) for i, room in enumerate(ROOMS)],
        compressed_tokens,
        picked_specialists.T,
        gating_shares.T,
        seat_limits.reshape(1, -1),
        raising_factors,
        lowering_factors,
        result_cotangent,
    )
    vmem = pl.BlockSpec(memory_space=pltpu.VMEM)
    results = (combined, latent_grad, prob_grad, up_grad, down_grad)
    combined, latent_grad, prob_grad, up_grad, down_grad = pl.pallas_call(
        store_kernel,
        out_shape=tuple(jax.ShapeDtypeStruct(r.shape, r.dtype) for r in results),
        in_specs=[vmem] * 5,
        out_specs=[vmem] * 5,
        name="store_results",
    )(*results)
    return combined, latent_grad, prob_grad.T, up_grad, down_grad


def solution(mesh):
    in_specs = (
        P(("dp", "expert"), None),
        P(("dp", "expert"), None),
        P(("dp", "expert"), None),
        P(),
        P("expert", "dp", None),
        P("expert", "dp", None),
        P(("dp", "expert"), None),
    )
    out_specs = (
        P(("dp", "expert"), None),
        P(("dp", "expert"), None),
        P(("dp", "expert"), None),
        P("expert", "dp", None),
        P("expert", "dp", None),
    )
    return jax.shard_map(body, mesh=mesh, in_specs=in_specs, out_specs=out_specs, check_vma=False)
```

```python
import functools

import jax
import jax.numpy as jnp
from jax import lax
from jax.experimental import pallas as pl
from jax.experimental.pallas import tpu as pltpu
from jax.sharding import PartitionSpec as P

DP_GRID = (4, 4)
EXPERT_GRID = (8, 4, 2)
SEATS = 8
ROOMS = (104, 112, 128)
PAIR = 2 * SEATS
COLUMNS = 256
CHUNKS = 2
MESH = pl.DeviceIdType.MESH
BF16 = jnp.bfloat16
F32 = jnp.float32


def dot(a, b):
    return jnp.dot(a, b, preferred_element_type=F32)


def dot_nt(a, b):
    return lax.dot_general(a, b, (((1,), (1,)), ((), ())), preferred_element_type=F32)


def dot_tn(a, b):
    return lax.dot_general(a, b, (((0,), (0,)), ((), ())), preferred_element_type=F32)


def parts_of(values):
    first = values.astype(BF16)
    rest = values - first.astype(F32)
    second = rest.astype(BF16)
    third = (rest - second.astype(F32)).astype(BF16)
    return first, second, third


def paired(upper, lower, blocks):
    width = upper.shape[-1]
    return jnp.concatenate(
        [upper.reshape(blocks, SEATS, width), lower.reshape(blocks, SEATS, width)], axis=1
    ).astype(BF16)


def unpaired(blocks):
    count, _, width = blocks.shape
    wide = blocks.astype(F32)
    return (
        wide[:, :SEATS].reshape(count * SEATS, width),
        wide[:, SEATS:].reshape(count * SEATS, width),
    )


def kernel(
    room,
    tok_hbm, cot_hbm, up_hbm, down_hbm, pick_hbm, share_hbm, limit_hbm,
    comb_ref, lat_ref, prob_ref, up_grad_ref, down_grad_ref,
    weights, tok, cot, pick_ref, share_ref, limit_ref, own_out, outbox, middle, inbox, reply, gather, packed, own_home, home,
    place, place_t, unfold, unfolded, cot_rows, row_share, xs, gs, hs, acts, partial, x_in, z_out, z_in,
    load_sem, ag_z_send, ag_z_recv, ag_x_send, ag_x_recv,
    out_z_send, out_z_recv, out_y_send, out_y_recv, out_self,
    back_y_send, back_y_recv, back_z_send, back_z_recv, back_self,
    rs_x_send, rs_x_recv, rs_z_send, rs_z_recv,
):
    runs, wide = DP_GRID
    ys, stretches, cores = EXPERT_GRID
    experts = ys * stretches * cores
    members = ys * cores
    tokens, lat = tok.shape
    top = pick_ref.shape[0]
    hid = weights.shape[-1]
    group_rows = members * SEATS
    near_slots = members * SEATS
    slots = place.shape[0]

    dp = lax.axis_index("dp")
    me = lax.axis_index("expert")
    run, across = dp // wide, dp % wide
    my_stretch = (me // cores) % stretches
    my_member = (me // (stretches * cores)) * cores + me % cores

    def run_peer(j):
        return {"dp": lax.rem(run + j, runs) * wide + across}

    def wide_peer(j):
        return {"dp": run * wide + lax.rem(across + j, wide)}

    def expert_of(stretch, member):
        return ((member // cores) * stretches + stretch) * cores + member % cores

    def member_peer(i):
        return {"expert": expert_of(my_stretch, lax.rem(my_member + i, members))}

    def stretch_peer(j):
        return {"expert": expert_of(lax.rem(my_stretch + j, stretches), my_member)}

    def steps_to(expert):
        member = expert // (stretches * cores) * cores + expert % cores
        return (
            (expert // cores + stretches - my_stretch) % stretches,
            (member + members - my_member) % members,
        )

    def remote(src, dst, send_sem, recv_sem, peer):
        return pltpu.make_async_remote_copy(
            src_ref=src, dst_ref=dst, send_sem=send_sem, recv_sem=recv_sem,
            device_id=peer, device_id_type=MESH,
        )

    def wait_bytes(ref, sem):
        pltpu.make_async_copy(ref, ref, sem).wait()

    loads = [
        pltpu.make_async_copy(src, dst, load_sem.at[i])
        for i, (src, dst) in enumerate(
            (
                (up_hbm.at[0], weights.at[0, run, across]),
                (down_hbm.at[0], weights.at[1, run, across]),
                (pick_hbm, pick_ref),
                (share_hbm, share_ref),
                (limit_hbm, limit_ref),
                (tok_hbm, tok),
                (cot_hbm, cot),
            )
        )
    ]
    for load in loads:
        load.start()

    barrier = pltpu.get_barrier_semaphore()
    peers = [run_peer(j) for j in range(1, runs)] + [wide_peer(j) for j in range(1, wide)]
    peers += [stretch_peer(j) for j in range(1, stretches)]
    for peer in peers:
        pl.semaphore_signal(barrier, inc=1, device_id=peer, device_id_type=MESH)

    def greet(i, carry):
        pl.semaphore_signal(barrier, inc=1, device_id=member_peer(i), device_id_type=MESH)
        return carry

    lax.fori_loop(1, members, greet, 0)

    for load in loads[2:5]:
        load.wait()

    picks = pick_ref[...]
    shares = share_ref[...]
    expert_row = lax.broadcasted_iota(jnp.int32, (experts, tokens), 0)
    named = jnp.zeros((experts, tokens), F32)
    weight = jnp.zeros((experts, tokens), F32)
    for k in range(top):
        hit = picks[k : k + 1] == expert_row
        named = jnp.where(hit, 1.0, named)
        weight = jnp.where(hit, shares[k : k + 1], weight)
    earlier = (
        lax.broadcasted_iota(jnp.int32, (tokens, tokens), 0)
        < lax.broadcasted_iota(jnp.int32, (tokens, tokens), 1)
    ).astype(BF16)
    position = dot(named.astype(BF16), earlier)
    square = lax.broadcasted_iota(jnp.int32, (experts, experts), 0) == lax.broadcasted_iota(
        jnp.int32, (experts, experts), 1
    )
    limit_row = limit_ref[...].astype(F32)
    limit = jnp.sum(jnp.where(square, limit_row, 0.0), axis=1, keepdims=True)
    seat = jnp.where((named > 0.0) & (position < limit), position, -1.0).astype(BF16)
    across_stretch, along_members = steps_to(lax.broadcasted_iota(jnp.int32, (1, experts), 1))
    down_stretch, down_members = steps_to(lax.broadcasted_iota(jnp.int32, (experts, 1), 0))
    ahead = (down_stretch == across_stretch) & (down_members < along_members)
    offset = jnp.sum(jnp.where(ahead, limit, 0.0), axis=0, keepdims=True)
    first_slot = jnp.where(
        across_stretch == 0,
        (along_members * SEATS).astype(F32),
        (near_slots + (across_stretch - 1) * room).astype(F32) + offset,
    )
    slot = lax.broadcasted_iota(jnp.int32, (slots, experts), 0).astype(F32)
    slot_expert = (slot >= first_slot) & (slot < first_slot + limit_row)
    taken = jnp.sum(jnp.where(slot_expert, 1.0, 0.0), axis=1, keepdims=True)
    slot_seat = jnp.sum(jnp.where(slot_expert, slot - first_slot, 0.0), axis=1, keepdims=True)
    slot_seat = jnp.where(taken > 0.0, slot_seat, -2.0)
    place[...] = (dot(slot_expert.astype(BF16), seat) == slot_seat).astype(BF16)
    row = lax.broadcasted_iota(jnp.int32, (members * PAIR, experts), 0)
    row_expert = (across_stretch == 0) & (along_members == row // PAIR)
    row_first = jnp.sum(jnp.where(row_expert, offset, 0.0), axis=1, keepdims=True)
    row_limit = jnp.sum(jnp.where(row_expert, limit_row, 0.0), axis=1, keepdims=True)
    row = lax.broadcasted_iota(jnp.int32, (members * PAIR, 1), 0)
    row_seat = (row % SEATS).astype(F32)
    row_source = jnp.where(
        row_seat < row_limit,
        ((row % PAIR) // SEATS * room).astype(F32) + row_first + row_seat,
        -1.0,
    )
    packed_row = lax.broadcasted_iota(jnp.int32, (members * PAIR, 2 * room), 1).astype(F32)
    unfold[...] = (packed_row == row_source).astype(BF16)

    loads[0].wait()
    loads[1].wait()
    pl.semaphore_wait(barrier, len(peers) + members - 1)

    z_copies = [
        [
            remote(
                weights.at[w, run, across], weights.at[w, run, across],
                ag_z_send.at[w, j], ag_z_recv.at[w, j], run_peer(j),
            )
            for j in range(1, runs)
        ]
        for w in range(2)
    ]

    def fan_out(w, block):
        for j in range(1, wide):
            part = weights.at[w, block, across]
            remote(part, part, ag_x_send.at[w], ag_x_recv.at[w], wide_peer(j)).start()

    def pass_on(w):
        for j in range(1, runs):
            z_copies[w][j - 1].wait_recv()
            fan_out(w, lax.rem(run + runs - j, runs))

    for copy in z_copies[0]:
        copy.start()
    for w in range(2):
        fan_out(w, run)

    loads[5].wait()
    loads[6].wait()
    x_rows = dot(place[...], tok[...])
    c_rows = dot(place[...], cot[...])
    cot_rows[...] = c_rows.astype(BF16)
    per_expert = sum(dot_nt(place[...], part) for part in parts_of(weight))
    slot_share = jnp.sum(jnp.where(slot_expert, per_expert, 0.0), axis=1, keepdims=True)
    row_share[...] = slot_share
    g_rows = slot_share * c_rows
    own_out[...] = paired(x_rows[:near_slots], g_rows[:near_slots], members)
    for j in range(1, stretches):
        first = near_slots + (j - 1) * room
        outbox[j - 1] = jnp.concatenate(
            [x_rows[first : first + room], g_rows[first : first + room]], axis=0
        ).astype(BF16)

    def spread(source, there):
        pltpu.make_async_copy(source.at[0], inbox.at[there, 0], out_self.at[there]).start()

        def send(i, carry):
            remote(
                source.at[i], inbox.at[there, members - i],
                out_y_send, out_y_recv.at[there], member_peer(i),
            ).start()
            return carry

        lax.fori_loop(1, members, send, 0)

    order = sorted(range(1, stretches), key=lambda j: min(j, stretches - j))
    near, far = order[:-1], order[-1]

    def set_out(j):
        remote(
            outbox.at[j - 1], middle.at[j - 1], out_z_send, out_z_recv.at[j], stretch_peer(j)
        ).start()

    for j in near:
        set_out(j)
    spread(own_out, 0)
    pass_on(0)
    for copy in z_copies[1]:
        copy.start()

    def arrive(j):
        wait_bytes(middle.at[j - 1], out_z_recv.at[j])

    def forward(j):
        blocks = dot(unfold[...], middle[j - 1]).astype(BF16)
        unfolded[j - 1] = blocks.reshape(unfolded.shape[1:])
        spread(unfolded.at[j - 1], (stretches - j) % stretches)

    def expert_step(there):
        pltpu.make_async_copy(inbox.at[there, 0], inbox.at[there, 0], out_self.at[there]).wait()
        wait_bytes(inbox.at[there, pl.ds(1, members - 1)], out_y_recv.at[there])
        rows = pl.ds(there * group_rows, group_rows)
        x_f32, g_f32 = unpaired(inbox[there])
        x = x_f32.astype(BF16)
        g = g_f32.astype(BF16)
        xs[rows] = x
        gs[rows] = g
        for column in range(0, hid, COLUMNS):
            columns = pl.ds(column, COLUMNS)
            active = jnp.maximum(dot(x, weights[0, :, :, :, columns].reshape(lat, COLUMNS)), 0.0)
            hidden_grad = dot(g, weights[1, :, :, :, columns].reshape(lat, COLUMNS))
            hs[rows, columns] = (active * active).astype(BF16)
            acts[rows, columns] = (2.0 * active * hidden_grad).astype(BF16)
        out = dot_nt(hs[rows], weights[1].reshape(lat, hid))
        row_grad = dot_nt(acts[rows], weights[0].reshape(lat, hid))
        reply[there] = paired(out, row_grad, members)

    def send_back(there):
        target = own_home if there == 0 else gather.at[there - 1]
        pltpu.make_async_copy(reply.at[there, 0], target.at[0], back_self.at[there]).start()

        def send(i, carry):
            remote(
                reply.at[there, i], target.at[members - i],
                back_y_send, back_y_recv.at[there], member_peer(i),
            ).start()
            return carry

        lax.fori_loop(1, members, send, 0)

    def gathered(there):
        target = own_home if there == 0 else gather.at[there - 1]
        pltpu.make_async_copy(target.at[0], target.at[0], back_self.at[there]).wait()
        wait_bytes(target.at[pl.ds(1, members - 1)], back_y_recv.at[there])

    def go_home(there):
        gathered(there)
        rows = gather[there - 1].reshape(members * PAIR, lat)
        packed[there - 1] = dot_tn(unfold[...], rows).astype(BF16)
        j = stretches - there
        remote(
            packed.at[there - 1], home.at[j - 1],
            back_z_send, back_z_recv.at[j], stretch_peer(there),
        ).start()

    for j in near:
        arrive(j)
        forward(j)
    pass_on(1)
    set_out(far)
    place_t[...] = place[...].T
    for w in range(2):
        wait_bytes(weights.at[w, :, pl.ds(0, wide - 1)], ag_x_recv.at[w])
    for j in near:
        expert_step(stretches - j)
        send_back(stretches - j)
    arrive(far)
    forward(far)
    expert_step(0)
    for j in near:
        go_home(stretches - j)
    send_back(0)
    expert_step(stretches - far)
    send_back(stretches - far)

    chunk_columns = hid // CHUNKS
    chunks = [
        (grad_ref, left, right, half * chunk_columns)
        for grad_ref, left, right in ((up_grad_ref, xs, acts), (down_grad_ref, gs, hs))
        for half in range(CHUNKS)
    ]
    for q, (_, left, right, start) in enumerate(chunks):
        for column in range(0, chunk_columns, COLUMNS):
            term = dot_tn(left[...], right[:, pl.ds(start + column, COLUMNS)])
            term = term.reshape(runs, wide, -1, COLUMNS).astype(BF16)
            partial[q, :, :, :, pl.ds(column, COLUMNS)] = term
        for j in range(1, wide):
            there = lax.rem(across + j, wide)
            remote(
                partial.at[q, :, there], x_in.at[q, j - 1],
                rs_x_send.at[q], rs_x_recv.at[q], wide_peer(j),
            ).start()
    go_home(stretches - far)
    for q in range(len(chunks)):
        wait_bytes(x_in.at[q], rs_x_recv.at[q])
        total = partial[q, :, across].astype(F32)
        for j in range(wide - 1):
            total += x_in[q, j].astype(F32)
        z_out[q] = total.astype(BF16)
        for j in range(1, runs):
            remote(
                z_out.at[q, lax.rem(run + j, runs)], z_in.at[q, j - 1],
                rs_z_send.at[q], rs_z_recv.at[q], run_peer(j),
            ).start()
    for q, (grad_ref, _, _, start) in enumerate(chunks):
        wait_bytes(z_in.at[q], rs_z_recv.at[q])
        total = z_out[q, run].astype(F32)
        for j in range(runs - 1):
            total += z_in[q, j].astype(F32)
        grad_ref[0, :, pl.ds(start, chunk_columns)] = total

    gathered(0)
    for j in range(1, stretches):
        wait_bytes(home.at[j - 1], back_z_recv.at[j])
    outs, row_grads = ([rows] for rows in unpaired(own_home[...]))
    for j in range(1, stretches):
        rows = home[j - 1].astype(F32)
        outs.append(rows[:room])
        row_grads.append(rows[room:])
    spare = slots - near_slots - (stretches - 1) * room
    if spare:
        outs.append(jnp.zeros((spare, lat), F32))
        row_grads.append(jnp.zeros((spare, lat), F32))
    out = jnp.concatenate(outs, axis=0)
    row_grad = jnp.concatenate(row_grads, axis=0)
    lat_ref[...] = dot(place_t[...], row_grad.astype(BF16)).astype(BF16)
    first, second, _ = parts_of(row_share[...] * out)
    comb_ref[...] = (dot(place_t[...], first) + dot(place_t[...], second)).astype(BF16)
    row_prob = jnp.sum(cot_rows[...].astype(F32) * out, axis=1, keepdims=True)
    by_expert = sum(
        dot_tn(part, place[...]) for part in parts_of(jnp.where(slot_expert, row_prob, 0.0))
    )
    for k in range(top):
        hit = picks[k : k + 1] == expert_row
        prob_ref[k : k + 1] = jnp.sum(jnp.where(hit, by_expert, 0.0), axis=0, keepdims=True)

    for w in range(2):
        for copy in z_copies[w]:
            copy.wait_send()
        wait_bytes(weights.at[w, :, pl.ds(0, wide - 1)], ag_x_send.at[w])
    wait_bytes(outbox, out_z_send)
    wait_bytes(inbox.at[:, pl.ds(1, members - 1)], out_y_send)
    wait_bytes(inbox.at[:, pl.ds(1, members - 1)], back_y_send)
    wait_bytes(home, back_z_send)
    for q in range(len(chunks)):
        wait_bytes(x_in.at[q], rs_x_send.at[q])
        wait_bytes(z_in.at[q], rs_z_send.at[q])


def layer(
    room,
    kernel_id,
    compressed_tokens,
    picked_specialists,
    gating_shares,
    seat_limits,
    raising_factors,
    lowering_factors,
    result_cotangent,
):
    runs, wide = DP_GRID
    ys, stretches, cores = EXPERT_GRID
    experts = ys * stretches * cores
    members = ys * cores
    tokens, lat = compressed_tokens.shape
    top = picked_specialists.shape[0]
    _, depth, hid = raising_factors.shape
    near_slots = members * SEATS
    slots = -(-(near_slots + (stretches - 1) * room) // 128) * 128
    rows = experts * SEATS
    vmem = pl.BlockSpec(memory_space=pltpu.VMEM)
    hbm = pl.BlockSpec(memory_space=pltpu.HBM)
    dma = pltpu.SemaphoreType.DMA
    blocks = pltpu.VMEM((stretches, members, PAIR, lat), BF16)
    far_blocks = pltpu.VMEM((stretches - 1, members, PAIR, lat), BF16)
    own_blocks = pltpu.VMEM((members, PAIR, lat), BF16)
    folded = pltpu.VMEM((stretches - 1, 2 * room, lat), BF16)
    outs = (
        jax.ShapeDtypeStruct((tokens, lat), BF16),
        jax.ShapeDtypeStruct((tokens, lat), BF16),
        jax.ShapeDtypeStruct((top, tokens), F32),
        jax.ShapeDtypeStruct((1, depth, hid), F32),
        jax.ShapeDtypeStruct((1, depth, hid), F32),
    )
    return pl.pallas_call(
        functools.partial(kernel, room),
        out_shape=outs,
        in_specs=[hbm] * 7,
        out_specs=[vmem] * 5,
        scratch_shapes=[
            pltpu.VMEM((2, runs, wide, depth, hid), BF16),
            pltpu.VMEM((tokens, lat), BF16),
            pltpu.VMEM((tokens, lat), BF16),
            pltpu.VMEM((top, tokens), jnp.int32),
            pltpu.VMEM((top, tokens), F32),
            pltpu.VMEM((1, experts), jnp.int32),
            own_blocks,
            folded,
            folded,
            blocks,
            blocks,
            far_blocks,
            folded,
            own_blocks,
            folded,
            pltpu.VMEM((slots, tokens), BF16),
            pltpu.VMEM((tokens, slots), BF16),
            pltpu.VMEM((members * PAIR, 2 * room), BF16),
            far_blocks,
            pltpu.VMEM((slots, lat), BF16),
            pltpu.VMEM((slots, 1), F32),
            pltpu.VMEM((rows, lat), BF16),
            pltpu.VMEM((rows, lat), BF16),
            pltpu.VMEM((rows, hid), BF16),
            pltpu.VMEM((rows, hid), BF16),
            pltpu.VMEM((2 * CHUNKS, runs, wide, depth, hid // CHUNKS), BF16),
            pltpu.VMEM((2 * CHUNKS, wide - 1, runs, depth, hid // CHUNKS), BF16),
            pltpu.VMEM((2 * CHUNKS, runs, depth, hid // CHUNKS), BF16),
            pltpu.VMEM((2 * CHUNKS, runs - 1, depth, hid // CHUNKS), BF16),
            dma((7,)),
            dma((2, runs)),
            dma((2, runs)),
            dma((2,)),
            dma((2,)),
            dma,
            dma((stretches,)),
            dma,
            dma((stretches,)),
            dma((stretches,)),
            dma,
            dma((stretches,)),
            dma,
            dma((stretches,)),
            dma((stretches,)),
            dma((2 * CHUNKS,)),
            dma((2 * CHUNKS,)),
            dma((2 * CHUNKS,)),
            dma((2 * CHUNKS,)),
        ],
        compiler_params=pltpu.CompilerParams(
            collective_id=kernel_id, has_side_effects=True, vmem_limit_bytes=60 * 1024 * 1024
        ),
        name="moe_layer",
    )(
        compressed_tokens,
        result_cotangent,
        raising_factors,
        lowering_factors,
        picked_specialists,
        gating_shares,
        seat_limits,
    )


def store_kernel(*refs):
    count = len(refs) // 2
    for src, dst in zip(refs[:count], refs[count:]):
        dst[...] = src[...]


def body(
    compressed_tokens,
    picked_specialists,
    gating_shares,
    seat_limits,
    raising_factors,
    lowering_factors,
    result_cotangent,
):
    ys, stretches, cores = EXPERT_GRID
    filled = jnp.sum(seat_limits.reshape(ys, stretches, cores), axis=(0, 2))
    choice = jnp.max(sum((filled > room).astype(jnp.int32) for room in ROOMS[:-1]))
    combined, latent_grad, prob_grad, up_grad, down_grad = lax.switch(
        choice,
        [functools.partial(layer, room, i) for i, room in enumerate(ROOMS)],
        compressed_tokens,
        picked_specialists.T,
        gating_shares.T,
        seat_limits.reshape(1, -1),
        raising_factors,
        lowering_factors,
        result_cotangent,
    )
    vmem = pl.BlockSpec(memory_space=pltpu.VMEM)
    results = (combined, latent_grad, prob_grad, up_grad, down_grad)
    combined, latent_grad, prob_grad, up_grad, down_grad = pl.pallas_call(
        store_kernel,
        out_shape=tuple(jax.ShapeDtypeStruct(r.shape, r.dtype) for r in results),
        in_specs=[vmem] * 5,
        out_specs=[vmem] * 5,
        name="store_results",
    )(*results)
    return combined, latent_grad, prob_grad.T, up_grad, down_grad


def solution(mesh):
    in_specs = (
        P(("dp", "expert"), None),
        P(("dp", "expert"), None),
        P(("dp", "expert"), None),
        P(),
        P("expert", "dp", None),
        P("expert", "dp", None),
        P(("dp", "expert"), None),
    )
    out_specs = (
        P(("dp", "expert"), None),
        P(("dp", "expert"), None),
        P(("dp", "expert"), None),
        P("expert", "dp", None),
        P("expert", "dp", None),
    )
    return jax.shard_map(body, mesh=mesh, in_specs=in_specs, out_specs=out_specs, check_vma=False)
```
